256 devices in a mesh: pipe: 8 (over x, core), expert: 32 (over z, y).
Axes of the slice: x: 4, y: 4, z: 8, core: 2. Of those that a mesh axis runs over, the one named last changes fastest.
Arguments:
- layer_input: bfloat16 [8, 8192, 3584], P('pipe', 'expert'), may hold values from -6 to 6
- out_grad: bfloat16 [8, 8192, 3584], P('pipe', 'expert'), may hold values from -6 to 6
- combine_weights: float32 [8, 8192, 8], P('pipe', 'expert'), may hold values from 0.05 to 1
- expert_ids: int32 [8, 8192, 8], P('pipe', 'expert'), may hold values from 0 to 255, as said below
- w_gate: bfloat16 [8, 3584, 4096], P('pipe', None, 'expert'), as said below
- w_up: bfloat16 [8, 3584, 4096], P('pipe', None, 'expert'), as said below
- w_down: bfloat16 [8, 4096, 3584], P('pipe', 'expert'), as said below
Outputs:
- input_grad: bfloat16 [8, 8192, 3584], P('pipe', 'expert')
- gate_grad: bfloat16 [8, 3584, 4096], P('pipe', None, 'expert')
- up_grad: bfloat16 [8, 3584, 4096], P('pipe', None, 'expert')
- down_grad: bfloat16 [8, 4096, 3584], P('pipe', 'expert')
The draws below stay inside these ranges and needn't reach their ends.
Inputs may be any that keep to these rules, and one draw needn't show every extreme that they name: `expert_ids`: each row names 8 different experts. Among the tokens of one device (one section, one aligned block of 256) each expert below 4 is named by 1 to 16 tokens; in each section one of these experts is named by exactly 16 tokens on every device. w_gate[p] equals w_gate[7 - p]. w_up[p] equals w_up[7 - p]. w_down[p] equals w_down[7 - p].
All inputs are finite; a program needn't handle non-finite values.
Results may differ from the reference program's by a relative error of at most 0.02.
Values may be sent and summed in bfloat16 or wider, within the bound.
A program may use at most 128 MiB of HBM per device.

```python
import jax
import jax.numpy as jnp
from jax import lax

D = 3584
FF = 1024
SPLIT = 8
ROUTED = 256
TOPK = 8
TOK_DEV = 256
CAP = 16
FF_DEV = 128
EF = 4
TOKENS = 8192
N_PIPE = 8
N_EXPERT = 32


def mirrored(key, row_count, col_count, fan_size):
    half_count = N_PIPE // 2
    drawn_half = jax.random.normal(key, (half_count, row_count, col_count), jnp.float32) * fan_size ** (-0.5)
    return jnp.concatenate([drawn_half, drawn_half[::-1]], axis=0).astype(jnp.bfloat16)


def draw_w_gate(key, part):
    key = jax.random.fold_in(key, 21)
    return mirrored(key, D, EF * FF, D)


def draw_w_up(key, part):
    key = jax.random.fold_in(key, 22)
    return mirrored(key, D, EF * FF, D)


def draw_w_down(key, part):
    key = jax.random.fold_in(key, 23)
    return mirrored(key, EF * FF, D, FF)


def draw_expert_ids(key, part):
    key = jax.random.fold_in(key, 11)
    key_full, key_count, key_order, key_other, key_shuffle = jax.random.split(key, 5)
    flight = N_EXPERT // SPLIT
    blocks = N_PIPE * N_EXPERT
    row_total = N_PIPE * TOKENS
    fullest = jax.random.randint(key_full, (N_PIPE, 1, 1), 0, flight)
    counts = jax.random.randint(key_count, (N_PIPE, N_EXPERT, flight), 1, CAP + 1)
    counts = jnp.where(jnp.arange(flight)[None, None, :] == fullest, CAP, counts)
    order_keys = jax.random.split(key_order, blocks * flight)
    orders = jax.vmap(lambda single_key: jax.random.permutation(single_key, TOK_DEV))(order_keys)
    ranks = jnp.argsort(orders, axis=1).reshape(N_PIPE, N_EXPERT, flight, TOK_DEV)
    chosen = ranks < counts[:, :, :, None]
    chosen = jnp.transpose(chosen, (0, 1, 3, 2)).reshape(row_total, flight)
    labels = jnp.where(chosen, jnp.arange(flight, dtype=jnp.int32)[None, :], ROUTED)
    labels = jnp.sort(labels, axis=1)
    labels = jnp.pad(labels, ((0, 0), (0, TOPK - flight)), constant_values=ROUTED)
    live_count = jnp.sum(chosen.astype(jnp.int32), axis=1, keepdims=True)
    others_count = ROUTED - flight
    scores = jax.random.randint(key_other, (row_total, others_count), 0, 2 ** 22) * others_count + jnp.arange(others_count, dtype=jnp.int32)[None, :]
    top_values, picked = lax.top_k(scores, TOPK)
    others = picked.astype(jnp.int32) + flight
    position = jnp.arange(TOPK, dtype=jnp.int32)[None, :]
    from_other = jnp.take_along_axis(others, jnp.clip(position - live_count, 0, TOPK - 1), axis=1)
    combined = jnp.where(position < live_count, labels, from_other)
    shuffle = jax.random.randint(key_shuffle, (row_total, TOPK), 0, 2 ** 20) * TOPK + position
    shuffle_values, slot_order = lax.top_k(shuffle, TOPK)
    result = jnp.take_along_axis(combined, slot_order.astype(jnp.int32), axis=1)
    return result.reshape(N_PIPE, TOKENS, TOPK).astype(jnp.int32)


def level_of(stream_key, dims, cuts, smallest, top_value):
    factor_of, own = 1.0, jax.random.fold_in(stream_key, 6)
    for dim, shards_of in cuts:
        heights = jnp.exp(jax.random.uniform(jax.random.fold_in(own, dim), (shards_of,), jnp.float32, smallest / len(cuts), top_value / len(cuts)))
        factor_of = factor_of * jnp.repeat(heights, dims[dim] // shards_of).reshape([-1 if axis == dim else 1 for axis in range(len(dims))])
    return factor_of


def noise(rng, dims, scale, reach, cuts=(), kind=jnp.bfloat16):
    level = level_of(rng, dims, cuts, -0.22, 0.18) if cuts else 1.0
    values = jax.random.normal(rng, dims, jnp.float32) * scale * level
    return jnp.minimum(jnp.maximum(values, -reach), reach).astype(kind)


def setup_inputs(seed: int = 0) -> dict:
    arg_keys = jax.random.split(jax.random.key(seed), 8)
    layer_input = noise(arg_keys[0], (N_PIPE, TOKENS, D), 1.0, 6.0, ((0, 8), (1, 32)))
    out_grad = noise(arg_keys[1], (N_PIPE, TOKENS, D), 1.0, 6.0, ((0, 8), (1, 32)))
    combine_weights = jnp.clip(0.05 + 0.95 * jax.random.uniform(arg_keys[2], (N_PIPE, TOKENS, TOPK), jnp.float32) ** level_of(arg_keys[2], (N_PIPE, TOKENS, TOPK), ((0, 8), (1, 32)), -0.2, 0.2), 0.05, 1.0)
    expert_ids = draw_expert_ids(jax.random.fold_in(arg_keys[7], 71), 0)
    w_gate = draw_w_gate(jax.random.fold_in(arg_keys[7], 71), 0)
    w_up = draw_w_up(jax.random.fold_in(arg_keys[7], 71), 0)
    w_down = draw_w_down(jax.random.fold_in(arg_keys[7], 71), 0)
    return dict(layer_input=layer_input, out_grad=out_grad, combine_weights=combine_weights, expert_ids=expert_ids, w_gate=w_gate, w_up=w_up, w_down=w_down)


def section_backward(section_args):
    layer_input, out_grad, combine_weights, expert_ids, w_gate, w_up, w_down = section_args
    block_input = layer_input.reshape(N_EXPERT, TOK_DEV, D)
    block_grad = out_grad.reshape(N_EXPERT, TOK_DEV, D)
    block_ids = expert_ids.reshape(N_EXPERT, TOK_DEV, TOPK)
    block_probs = combine_weights.reshape(N_EXPERT, TOK_DEV, TOPK)
    slot_rows = N_EXPERT * CAP
    token_grad = jnp.zeros((N_EXPERT, TOK_DEV, D), jnp.float32)
    gate_parts = []
    up_parts = []
    down_parts = []
    source_index = jnp.arange(N_EXPERT, dtype=jnp.int32)[:, None]
    for expert in range(EF):
        chosen = block_ids == expert
        selected = jnp.any(chosen, axis=2).astype(jnp.int32)
        weight_sel = jnp.sum(jnp.where(chosen, block_probs, jnp.float32(0.0)), axis=2)
        slots = (jnp.cumsum(selected, axis=1) - selected).astype(jnp.int32)
        placed = (selected[:, None, :] == 1) & (slots[:, None, :] == jnp.arange(CAP, dtype=jnp.int32)[None, :, None])
        place_float = placed.astype(jnp.float32)
        token_index = jnp.sum(jnp.where(placed, jnp.arange(TOK_DEV, dtype=jnp.int32)[None, None, :], 0), axis=2).astype(jnp.int32)
        valid = jnp.any(placed, axis=2)[:, :, None]
        rows_input = jnp.where(valid, block_input[source_index, token_index], jnp.zeros((), jnp.bfloat16)).reshape(slot_rows, D)
        rows_grad = jnp.where(valid, block_grad[source_index, token_index], jnp.zeros((), jnp.bfloat16)).reshape(slot_rows, D)
        slot_prob = jnp.sum(place_float * weight_sel[:, None, :], axis=2).reshape(slot_rows, 1)
        scaled = (slot_prob * rows_grad.astype(jnp.float32)).astype(jnp.bfloat16)
        gate_cols = w_gate[:, expert * FF:(expert + 1) * FF]
        up_cols = w_up[:, expert * FF:(expert + 1) * FF]
        down_rows = w_down[expert * FF:(expert + 1) * FF, :]
        pre_gate = jnp.dot(rows_input, gate_cols, preferred_element_type=jnp.float32)
        pre_up = jnp.dot(rows_input, up_cols, preferred_element_type=jnp.float32)
        sigmoid_gate = jax.nn.sigmoid(pre_gate)
        activated = pre_gate * sigmoid_gate
        hidden = (activated * pre_up).astype(jnp.bfloat16)
        d_hidden = jnp.dot(scaled, down_rows.T, preferred_element_type=jnp.float32)
        d_gate = (d_hidden * pre_up * sigmoid_gate * (1.0 + pre_gate * (1.0 - sigmoid_gate))).astype(jnp.bfloat16)
        d_up = (d_hidden * activated).astype(jnp.bfloat16)
        down_parts.append(jnp.dot(hidden.T, scaled, preferred_element_type=jnp.float32).astype(jnp.bfloat16))
        gate_parts.append(jnp.dot(rows_input.T, d_gate, preferred_element_type=jnp.float32).astype(jnp.bfloat16))
        up_parts.append(jnp.dot(rows_input.T, d_up, preferred_element_type=jnp.float32).astype(jnp.bfloat16))
        gate_pieces = gate_cols.astype(jnp.float32).reshape(D, SPLIT, FF_DEV)
        up_pieces = up_cols.astype(jnp.float32).reshape(D, SPLIT, FF_DEV)
        partial_value = jnp.einsum("rqf,dqf->rqd", d_gate.astype(jnp.float32).reshape(slot_rows, SPLIT, FF_DEV), gate_pieces)
        partial_value = partial_value + jnp.einsum("rqf,dqf->rqd", d_up.astype(jnp.float32).reshape(slot_rows, SPLIT, FF_DEV), up_pieces)
        partial_value = partial_value.astype(jnp.bfloat16)
        summed = jnp.sum(partial_value.astype(jnp.float32), axis=1).reshape(N_EXPERT, CAP, D)
        token_grad = token_grad + jnp.einsum("sct,scd->std", place_float, summed, precision=lax.Precision.HIGHEST)
    input_grad = token_grad.reshape(TOKENS, D).astype(jnp.bfloat16)
    return (input_grad, jnp.concatenate(gate_parts, axis=1), jnp.concatenate(up_parts, axis=1), jnp.concatenate(down_parts, axis=0))


def mirror_sum(section_grad):
    return (section_grad.astype(jnp.float32) + section_grad[::-1].astype(jnp.float32)).astype(jnp.bfloat16)


def reference(layer_input, out_grad, combine_weights, expert_ids, w_gate, w_up, w_down):
    input_grad, gate_section, up_section, down_section = lax.map(section_backward, (layer_input, out_grad, combine_weights, expert_ids, w_gate, w_up, w_down))
    return (input_grad, mirror_sum(gate_section), mirror_sum(up_section), mirror_sum(down_section))
```

```python
import jax
import jax.numpy as jnp
from jax import lax
from jax.experimental import pallas as pl
from jax.experimental.pallas import tpu as pltpu
from jax.sharding import PartitionSpec as P

MESH = pl.DeviceIdType.MESH
BF16 = jnp.bfloat16
F32 = jnp.float32

NY = 4
NZ = 8
EF = 4
CAP = 16
DELTA = (0, 1, 7, 2, 6, 3, 5, 4)
COLS = 256
ANY = pl.BlockSpec(memory_space=pl.ANY)
VMEM = pl.BlockSpec(memory_space=pltpu.VMEM)


def dot(a, b):
    return jnp.dot(a, b, preferred_element_type=F32)


def kernel(
    ids,
    probs,
    x_h,
    g_h,
    wg_h,
    wu_h,
    wd_h,
    ig_h,
    gg_h,
    ug_h,
    dg_h,
    tok,
    wgu,
    wd,
    wgut,
    wdt,
    pmat,
    pmat_t,
    wslot,
    s_own,
    s_mir,
    s_out,
    rows,
    pf,
    ps,
    pr,
    da,
    dat,
    go_g,
    go_u,
    go_d,
    pb,
    anti,
    near,
    fin,
    home,
    slots,
    slots_m,
    slots_o,
    out,
    lsem,
    bsem,
    zs,
    zr,
    ys,
    yr,
    fs,
    fr,
    xs,
    xr,
    cs,
    ans,
    anr,
    ns,
    nr,
    hs,
    hr,
    gs,
    gr,
    gl,
    ol,
):
    n_pipe = lax.axis_size("pipe")
    p = lax.axis_index("pipe")
    ex = lax.axis_index("expert")
    z = lax.div(ex, NY)
    y = lax.rem(ex, NY)
    tokens, half_width = tok.shape[1], tok.shape[2]
    n_cols = half_width // COLS
    half = lax.div(p, n_pipe // 2)
    col = pl.multiple_of(half * half_width, 128)
    ocol = pl.multiple_of((1 - half) * half_width, 128)
    mirror = (n_pipe - 1 - p, ex)
    y_up = (p, z * NY + lax.rem(y + 1, NY))
    y_dn = (p, z * NY + lax.rem(y + NY - 1, NY))

    def z_at(delta):
        return (p, lax.rem(z + delta, NZ) * NY + y)

    def remote(src, dst, send, recv, device):
        return pltpu.make_async_remote_copy(
            src_ref=src, dst_ref=dst, send_sem=send, recv_sem=recv, device_id=device, device_id_type=MESH
        )

    def cut(n):
        return pl.ds(pl.multiple_of(n * COLS, COLS), COLS)

    loads = [
        pltpu.make_async_copy(x_h.at[:, pl.ds(col, half_width)], tok.at[0], lsem.at[0]),
        pltpu.make_async_copy(g_h.at[:, pl.ds(col, half_width)], tok.at[1], lsem.at[1]),
        pltpu.make_async_copy(x_h.at[:, pl.ds(ocol, half_width)], tok.at[2], lsem.at[2]),
        pltpu.make_async_copy(g_h.at[:, pl.ds(ocol, half_width)], tok.at[3], lsem.at[3]),
        pltpu.make_async_copy(wg_h.at[pl.ds(col, half_width), :], wgu.at[:, pl.ds(0, 128)], lsem.at[4]),
        pltpu.make_async_copy(wu_h.at[pl.ds(col, half_width), :], wgu.at[:, pl.ds(128, 128)], lsem.at[5]),
        pltpu.make_async_copy(wd_h.at[:, pl.ds(col, half_width)], wd, lsem.at[6]),
    ]
    for c in loads:
        c.start()

    barrier = pltpu.get_barrier_semaphore()
    partners = [mirror, y_up, y_dn] + [z_at(d) for d in range(1, NZ)]
    for device in partners:
        pl.semaphore_signal(barrier, inc=1, device_id=device, device_id_type=MESH)

    lane = lax.broadcasted_iota(jnp.int32, (tokens, 128), 1)
    lane_expert = lax.div(lane, CAP)
    named = jnp.zeros((tokens, 128), F32)
    weight = jnp.zeros((tokens, 128), F32)
    for k in range(ids.shape[1]):
        hit = ids[:, k : k + 1] == lane_expert
        named = jnp.where(hit, 1.0, named)
        weight = jnp.where(hit, probs[:, k : k + 1], weight)
    named = jnp.where(lane < EF * CAP, named, 0.0)
    before = (
        lax.broadcasted_iota(jnp.int32, (tokens, tokens), 0) > lax.broadcasted_iota(jnp.int32, (tokens, tokens), 1)
    ).astype(F32)
    count = dot(before.astype(BF16), named.astype(BF16))
    placed = jnp.where(count == lax.rem(lane, CAP).astype(F32), named, 0.0)
    pmat_t[...] = placed.astype(BF16)
    pmat[...] = placed.T.astype(BF16)
    wslot[...] = jnp.sum((placed * weight).T, axis=1, keepdims=True)

    def gather(base, dst):
        def step(n, _):
            x_rows = dot(pmat[0 : EF * CAP, :], tok[base, :, cut(n)])
            dst[0, :, :, cut(n)] = x_rows.astype(BF16).reshape(EF, CAP, COLS)
            g_rows = dot(pmat[0 : EF * CAP, :], tok[base + 1, :, cut(n)]) * wslot[0 : EF * CAP, :]
            dst[1, :, :, cut(n)] = g_rows.astype(BF16).reshape(EF, CAP, COLS)
            return 0

        lax.fori_loop(0, n_cols, step, 0)

    loads[0].wait()
    loads[1].wait()
    gather(0, s_own)

    source = (s_own, s_mir)

    def z_send(r, s):
        tz = lax.rem(z + DELTA[s], NZ)
        return remote(
            source[r].at[:, lax.div(tz, 2)], rows.at[:, r, s, 0], zs.at[r, s], zr.at[r, s], z_at(DELTA[s])
        )

    def y_send(r, s, way):
        return remote(
            rows.at[:, r, s, 0], rows.at[:, r, s, 1 + way], ys.at[way, r, s], yr.at[way, r, s], (y_up, y_dn)[way]
        )

    def forward(r, s, way):
        return remote(
            rows.at[way, r, s, 1 + way], rows.at[way, r, s, 3], fs.at[way, r, s], fr.at[way, r, s], (y_up, y_dn)[way]
        )

    cross = remote(s_out, s_mir, cs.at[0], cs.at[1], mirror)

    pl.semaphore_wait(barrier, len(partners))
    steps = [(r, s) for r in range(2) for s in range(NZ)]
    z_order = [(r, s) for r, s in steps if s > 0]
    issued = 0

    def issue_z(upto):
        nonlocal issued
        while issued < min(upto, len(z_order)):
            z_send(*z_order[issued]).start()
            issued += 1

    issue_z(4)
    rows[:, 0, 0, 0] = s_own[:, lax.div(z, 2)]
    for way in range(2):
        y_send(0, 0, way).start()

    loads[2].wait()
    loads[3].wait()
    gather(2, s_out)
    cross.start()

    for c in loads[4:]:
        c.wait()
    for n in range(n_cols):
        wgut[:, n * COLS : (n + 1) * COLS] = wgu[n * COLS : (n + 1) * COLS, :].T
        wdt[n * COLS : (n + 1) * COLS, :] = wd[:, n * COLS : (n + 1) * COLS].T

    def partial_send(c):
        r, k = c // 4, c % 4
        there = (1 - r) * 4 + k
        return remote(ps.at[c], pr.at[there], xs.at[c], xr.at[there], mirror)

    def partial_recv(c):
        return remote(ps.at[c], pr.at[c], xs.at[c], xr.at[c], mirror)

    def products(c):
        r, k = c // 4, c % 4
        gu = dot(rows[0, r, 2 * k : 2 * k + 2].reshape(128, half_width), wgu[...])
        dh = dot(rows[1, r, 2 * k : 2 * k + 2].reshape(128, half_width), wdt[...])
        pf[c, :, 0:256] = gu
        pf[c, :, 256:384] = dh
        ps[c, :, 0:256] = gu.astype(BF16)
        ps[c, :, 256:384] = dh.astype(BF16)
        partial_send(c).start()

    def activations(c):
        r, k = c // 4, c % 4
        partial_recv(c).wait_recv()
        full = pf[c] + pr[c].astype(F32)
        gate, up, dh = full[:, 0:128], full[:, 128:256], full[:, 256:384]
        sig = jax.nn.sigmoid(gate)
        act = gate * sig
        hidden = act * up
        d_gate = dh * up * sig * (1.0 + gate * (1.0 - sig))
        d_up = dh * act
        da[r, 2 * k : 2 * k + 2, :, :, 0:128] = d_gate.astype(BF16).reshape(2, NY, CAP, 128)
        da[r, 2 * k : 2 * k + 2, :, :, 128:256] = d_up.astype(BF16).reshape(2, NY, CAP, 128)
        span = slice(c * 128, (c + 1) * 128)
        dat[0:128, span] = d_gate.T.astype(BF16)
        dat[128:256, span] = d_up.T.astype(BF16)
        dat[256:384, span] = hidden.T.astype(BF16)

    def forward_step(i):
        r, s = steps[i]
        for way in range(2):
            y_send(r, s, way).wait_recv()
            forward(r, s, way).start()

    def finish_step(i):
        r, s = steps[i]
        for way in range(2):
            forward(r, s, way).wait_recv()

    def chunk_done(c):
        products(c)
        if c >= 4:
            activations(c)
        if c >= 5:
            activations(c - 5)

    for i, (r, s) in enumerate(steps):
        if i > 0:
            if s > 0:
                z_send(r, s).wait_recv()
            else:
                rows[:, r, 0, 0] = s_mir[:, lax.div(z, 2)]
            for way in range(2):
                y_send(r, s, way).start()
        if i == 3:
            cross.wait_recv()
        issue_z(i + 5)
        if i >= 1:
            forward_step(i - 1)
        if i >= 2:
            finish_step(i - 2)
            if (i - 2) % 2 == 1:
                chunk_done((i - 2) // 2)
    last = len(steps) - 1
    forward_step(last)
    finish_step(last - 1)
    finish_step(last)
    chunk_done(7)
    activations(3)

    def grad_copies(n):
        here = pl.ds(pl.multiple_of(col + n * COLS, 128), COLS)
        span = pl.ds(n * COLS, COLS)
        pairs = (
            (go_g.at[span, :], gg_h.at[here, :]),
            (go_u.at[span, :], ug_h.at[here, :]),
            (go_d.at[n], dg_h.at[:, here]),
        )
        for j, (src, dst) in enumerate(pairs):
            yield remote(src, dst, gs.at[n, j], gr.at[n, j], mirror), pltpu.make_async_copy(src, dst, gl.at[n, j])

    def grad_recv(n, j):
        there = pl.ds(pl.multiple_of(ocol + n * COLS, 128), COLS)
        span = pl.ds(n * COLS, COLS)
        src, dst = (
            (go_g.at[span, :], gg_h.at[there, :]),
            (go_u.at[span, :], ug_h.at[there, :]),
            (go_d.at[n], dg_h.at[:, there]),
        )[j]
        return remote(src, dst, gs.at[n, j], gr.at[n, j], mirror)

    def grads(n):
        span = slice(n * COLS, (n + 1) * COLS)
        gu = dot(dat[0:256, :], rows[0, :, :, :, :, span].reshape(1024, COLS)).T
        go_g[span, :] = gu[:, 0:128].astype(BF16)
        go_u[span, :] = gu[:, 128:256].astype(BF16)
        go_d[n] = dot(dat[256:384, :], rows[1, :, :, :, :, span].reshape(1024, COLS)).astype(BF16)
        for far, local in grad_copies(n):
            far.start()
            local.start()

    quarter = half_width // 2

    def anti_send(g, way):
        return remote(
            pb.at[:, pl.ds(2 * g, 2), 3, :, pl.ds(way * quarter, quarter)],
            anti.at[way, :, pl.ds(2 * g, 2)],
            ans.at[way, g],
            anr.at[way, g],
            (y_up, y_dn)[way],
        )

    def near_send(g, way):
        return remote(
            pb.at[:, pl.ds(2 * g, 2), 2 - way],
            near.at[way, :, pl.ds(2 * g, 2)],
            ns.at[way, g],
            nr.at[way, g],
            (y_up, y_dn)[way],
        )

    def parts(g):
        span = slice(2 * g, 2 * g + 2)
        lhs = da[:, span].reshape(256, 256)

        def step(n, _):
            part = dot(lhs, wgut[:, cut(n)])
            pb[:, span, :, :, cut(n)] = part.astype(BF16).reshape(2, 2, NY, CAP, COLS)
            return 0

        lax.fori_loop(0, n_cols, step, 0)
        for way in range(2):
            anti_send(g, way).start()

    def nears(g):
        span = slice(2 * g, 2 * g + 2)
        for way in range(2):
            anti_send(g, way).wait_recv()
            part = slice(way * quarter, (way + 1) * quarter)
            total = pb[:, span, 2 - way, :, part].astype(F32) + anti[way, :, span].astype(F32)
            pb[:, span, 2 - way, :, part] = total.astype(BF16)
            near_send(g, way).start()

    def home_send(s):
        back = NZ - DELTA[s]
        return remote(fin.at[s], home.at[z], hs.at[s], hr.at[s], z_at(back))

    def home_recv(s):
        return remote(fin.at[s], home.at[lax.rem(z + DELTA[s], NZ)], hs.at[s], hr.at[s], z_at(NZ - DELTA[s]))

    def sums(g):
        span = slice(2 * g, 2 * g + 2)
        for way in range(2):
            near_send(g, way).wait_recv()
        for s in range(2 * g, 2 * g + 2):
            total = pb[:, s, 0].astype(F32) + near[0, :, s].astype(F32) + near[1, :, s].astype(F32)
            if s == 0:
                home[z] = total.astype(BF16)
            else:
                fin[s] = total.astype(BF16)
                home_send(s).start()

    parts(3)
    grads(0)
    parts(2)
    nears(3)
    grads(1)
    parts(1)
    nears(2)
    grads(2)
    parts(0)
    nears(1)
    grads(3)
    sums(3)
    nears(0)
    grads(4)
    sums(2)
    grads(5)
    sums(1)
    grads(6)
    sums(0)

    for s in range(1, NZ):
        home_recv(s).wait_recv()
    for e in range(EF):
        both = home[2 * e].astype(F32) + home[2 * e + 1].astype(F32)
        slots[e * CAP : (e + 1) * CAP, :] = both[0].astype(BF16)
        slots_m[e * CAP : (e + 1) * CAP, :] = both[1].astype(BF16)
    swap = remote(slots_m, slots_o, cs.at[2], cs.at[3], mirror)
    swap.start()

    def place(index, value):
        def step(n, _):
            got = dot(pmat_t[:, 0 : EF * CAP], value[:, cut(n)])
            out[index, :, cut(n)] = got.astype(BF16)
            return 0

        lax.fori_loop(0, n_cols, step, 0)

    place(0, slots)
    first = pltpu.make_async_copy(out.at[0], ig_h.at[:, pl.ds(col, half_width)], ol.at[0])
    first.start()
    swap.wait_recv()
    place(1, slots_o)
    second = pltpu.make_async_copy(out.at[1], ig_h.at[:, pl.ds(ocol, half_width)], ol.at[1])
    second.start()

    for n in range(n_cols):
        for j in range(3):
            grad_recv(n, j).wait_recv()
        for far, local in grad_copies(n):
            far.wait_send()
            local.wait()
    for r, s in steps:
        if s > 0:
            z_send(r, s).wait_send()
        for way in range(2):
            y_send(r, s, way).wait_send()
            forward(r, s, way).wait_send()
    for c in range(8):
        partial_send(c).wait_send()
    for g in range(4):
        for way in range(2):
            anti_send(g, way).wait_send()
            near_send(g, way).wait_send()
    for s in range(1, NZ):
        home_send(s).wait_send()
    cross.wait_send()
    swap.wait_send()
    first.wait()
    second.wait()


def body(layer_input, out_grad, combine_weights, expert_ids, w_gate, w_up, w_down):
    tokens, width = layer_input.shape[1:]
    h = width // 2
    n_cols = h // COLS
    dma = pltpu.SemaphoreType.DMA
    outs = pl.pallas_call(
        kernel,
        out_shape=(
            jax.ShapeDtypeStruct((tokens, width), BF16),
            jax.ShapeDtypeStruct((width, 128), BF16),
            jax.ShapeDtypeStruct((width, 128), BF16),
            jax.ShapeDtypeStruct((128, width), BF16),
        ),
        in_specs=[VMEM, VMEM, ANY, ANY, ANY, ANY, ANY],
        out_specs=(ANY, ANY, ANY, ANY),
        scratch_shapes=[
            pltpu.VMEM((4, tokens, h), BF16),
            pltpu.VMEM((h, 256), BF16),
            pltpu.VMEM((128, h), BF16),
            pltpu.VMEM((256, h), BF16),
            pltpu.VMEM((h, 128), BF16),
            pltpu.VMEM((128, tokens), BF16),
            pltpu.VMEM((tokens, 128), BF16),
            pltpu.VMEM((128, 1), F32),
            pltpu.VMEM((2, EF, CAP, h), BF16),
            pltpu.VMEM((2, EF, CAP, h), BF16),
            pltpu.VMEM((2, EF, CAP, h), BF16),
            pltpu.VMEM((2, 2, NZ, NY, CAP, h), BF16),
            pltpu.VMEM((8, 128, 384), F32),
            pltpu.VMEM((8, 128, 384), BF16),
            pltpu.VMEM((8, 128, 384), BF16),
            pltpu.VMEM((2, NZ, NY, CAP, 256), BF16),
            pltpu.VMEM((384, 1024), BF16),
            pltpu.VMEM((h, 128), BF16),
            pltpu.VMEM((h, 128), BF16),
            pltpu.VMEM((n_cols, 128, COLS), BF16),
            pltpu.VMEM((2, NZ, NY, CAP, h), BF16),
            pltpu.VMEM((2, 2, NZ, CAP, h // 2), BF16),
            pltpu.VMEM((2, 2, NZ, CAP, h), BF16),
            pltpu.VMEM((NZ, 2, CAP, h), BF16),
            pltpu.VMEM((NZ, 2, CAP, h), BF16),
            pltpu.VMEM((EF * CAP, h), BF16),
            pltpu.VMEM((EF * CAP, h), BF16),
            pltpu.VMEM((EF * CAP, h), BF16),
            pltpu.VMEM((2, tokens, h), BF16),
            dma((7,)),
            dma((1,)),
            dma((2, NZ)),
            dma((2, NZ)),
            dma((2, 2, NZ)),
            dma((2, 2, NZ)),
            dma((2, 2, NZ)),
            dma((2, 2, NZ)),
            dma((8,)),
            dma((8,)),
            dma((4,)),
            dma((2, 4)),
            dma((2, 4)),
            dma((2, 4)),
            dma((2, 4)),
            dma((NZ,)),
            dma((NZ,)),
            dma((n_cols, 3)),
            dma((n_cols, 3)),
            dma((n_cols, 3)),
            dma((2,)),
        ],
        compiler_params=pltpu.CompilerParams(
            collective_id=0, has_side_effects=True, vmem_limit_bytes=56 * 1024 * 1024
        ),
    )(
        expert_ids[0],
        combine_weights[0],
        layer_input[0],
        out_grad[0],
        w_gate[0],
        w_up[0],
        w_down[0],
    )
    return tuple(o[None] for o in outs)


def solution(mesh):
    return jax.shard_map(
        body,
        mesh=mesh,
        in_specs=(
            P("pipe", "expert", None),
            P("pipe", "expert", None),
            P("pipe", "expert", None),
            P("pipe", "expert", None),
            P("pipe", None, "expert"),
            P("pipe", None, "expert"),
            P("pipe", "expert", None),
        ),
        out_specs=(
            P("pipe", "expert", None),
            P("pipe", None, "expert"),
            P("pipe", None, "expert"),
            P("pipe", "expert", None),
        ),
        check_vma=False,
    )
```

```python
import jax
import jax.numpy as jnp
from jax import lax
from jax.experimental import pallas as pl
from jax.experimental.pallas import tpu as pltpu
from jax.sharding import PartitionSpec as P

MESH = pl.DeviceIdType.MESH
BF16 = jnp.bfloat16
F32 = jnp.float32

NY = 4
NZ = 8
EF = 4
AHEAD = 3
CROSS_AT = 5
HANDED = ((0, 0), (0, 1), (0, 2), (0, 3), (1, 1), (1, 2))
RELAYED = ((0, 2), (0, 3), (1, 2), (1, 3))
ORDER = ((0, 2, 1, 4, 3, 6, 5, 7), (2, 4, 3, 6, 5, 0, 7, 1))
CAP = 16
COLS = 256
ANY = pl.BlockSpec(memory_space=pl.ANY)
VMEM = pl.BlockSpec(memory_space=pltpu.VMEM)


def dot(a, b):
    return jnp.dot(a, b, preferred_element_type=F32)


def kernel(
    ids,
    probs,
    x_h,
    g_h,
    wg_h,
    wu_h,
    wd_h,
    so_h,
    pm_h,
    gg_h,
    ug_h,
    dg_h,
    tok,
    wgu,
    wd,
    wgut,
    wdt,
    pmat,
    pmat_t,
    wslot,
    s_own,
    s_mir,
    s_out,
    rows,
    pf,
    ps,
    pr,
    da,
    dat,
    go_g,
    go_u,
    go_d,
    pb,
    anti,
    near,
    fin,
    home,
    slots,
    slots_m,
    lsem,
    zs,
    zr,
    c0s,
    c0r,
    c3s,
    c3r,
    ys,
    yr,
    fs,
    fr,
    xs,
    xr,
    cs,
    ss,
    sr,
    ans,
    anr,
    ns,
    nr,
    hs,
    hr,
    gs,
    gr,
    gl,
    ol,
):
    n_pipe = lax.axis_size("pipe")
    p = lax.axis_index("pipe")
    ex = lax.axis_index("expert")
    z = lax.div(ex, NY)
    y = lax.rem(ex, NY)
    tokens, half_width = tok.shape[1], tok.shape[2]
    n_cols = half_width // COLS
    half = lax.div(p, n_pipe // 2)
    col = pl.multiple_of(half * half_width, 128)
    ocol = pl.multiple_of((1 - half) * half_width, 128)
    mirror = (n_pipe - 1 - p, ex)
    y_up = (p, z * NY + lax.rem(y + 1, NY))
    y_dn = (p, z * NY + lax.rem(y + NY - 1, NY))

    odd = lax.rem(z, 2)
    sign = 2 * odd - 1

    def z_at(delta):
        return (p, lax.rem(z + delta + NZ, NZ) * NY + y)

    pair = z_at(-sign)

    def toward(s):
        delta = (1 - 2 * lax.rem(z + s // 2, 2)) * (s // 2 + s % 2)
        return delta, lax.div(lax.rem(z + delta + NZ, NZ), 2)

    def remote(src, dst, send, recv, device):
        return pltpu.make_async_remote_copy(
            src_ref=src, dst_ref=dst, send_sem=send, recv_sem=recv, device_id=device, device_id_type=MESH
        )

    def cut(n):
        return pl.ds(pl.multiple_of(n * COLS, COLS), COLS)

    loads = [
        pltpu.make_async_copy(x_h.at[:, pl.ds(col, half_width)], tok.at[0], lsem.at[0]),
        pltpu.make_async_copy(g_h.at[:, pl.ds(col, half_width)], tok.at[1], lsem.at[1]),
        pltpu.make_async_copy(x_h.at[:, pl.ds(ocol, half_width)], tok.at[2], lsem.at[2]),
        pltpu.make_async_copy(g_h.at[:, pl.ds(ocol, half_width)], tok.at[3], lsem.at[3]),
        pltpu.make_async_copy(wg_h.at[pl.ds(col, half_width), :], wgu.at[:, pl.ds(0, 128)], lsem.at[4]),
        pltpu.make_async_copy(wu_h.at[pl.ds(col, half_width), :], wgu.at[:, pl.ds(128, 128)], lsem.at[5]),
        pltpu.make_async_copy(wd_h.at[:, pl.ds(col, half_width)], wd, lsem.at[6]),
    ]
    for c in loads:
        c.start()

    barrier = pltpu.get_barrier_semaphore()
    partners = [mirror, y_up, y_dn] + [z_at(d) for d in range(1, NZ)]
    for device in partners:
        pl.semaphore_signal(barrier, inc=1, device_id=device, device_id_type=MESH)

    row = lax.broadcasted_iota(jnp.int32, (128, tokens), 0)
    row_expert = lax.div(row, CAP)
    named = jnp.zeros((128, tokens), F32)
    weight = jnp.zeros((128, tokens), F32)
    for k in range(ids.shape[0]):
        hit = ids[k : k + 1, :] == row_expert
        named = jnp.where(hit, 1.0, named)
        weight = jnp.where(hit, probs[k : k + 1, :], weight)
    named = jnp.where(row < EF * CAP, named, 0.0)
    before = (
        lax.broadcasted_iota(jnp.int32, (tokens, tokens), 0) < lax.broadcasted_iota(jnp.int32, (tokens, tokens), 1)
    ).astype(F32)
    count = dot(named.astype(BF16), before.astype(BF16))
    placed = jnp.where(count == lax.rem(row, CAP).astype(F32), named, 0.0)
    pmat[...] = placed.astype(BF16)
    pmat_t[...] = placed.T.astype(BF16)
    wslot[...] = jnp.sum(placed * weight, axis=1, keepdims=True)
    save = pltpu.make_async_copy(pmat_t, pm_h, ol.at[0])
    save.start()

    def gather(base, dst):
        def step(n, _):
            x_rows = dot(pmat[0 : EF * CAP, :], tok[base, :, cut(n)])
            dst[0, :, :, cut(n)] = x_rows.astype(BF16).reshape(EF, CAP, COLS)
            g_rows = dot(pmat[0 : EF * CAP, :], tok[base + 1, :, cut(n)]) * wslot[0 : EF * CAP, :]
            dst[1, :, :, cut(n)] = g_rows.astype(BF16).reshape(EF, CAP, COLS)
            return 0

        lax.fori_loop(0, n_cols, step, 0)

    loads[0].wait()
    loads[1].wait()
    gather(0, s_own)

    source = (s_own, s_mir)

    def z_send(r, s):
        delta, expert = toward(s)
        return remote(source[r].at[:, expert], rows.at[:, r, s, 0], zs.at[r, s], zr.at[r, s], z_at(delta))

    def relay(r, j):
        return remote(rows.at[:, r, 2 * j, 0], rows.at[:, r, 2 * j + 1, 0], c0s.at[r, j], c0r.at[r, j], pair)

    def y_send(r, s, way):
        return remote(
            rows.at[:, r, s, 0], rows.at[:, r, s, 1 + way], ys.at[way, r, s], yr.at[way, r, s], (y_up, y_dn)[way]
        )

    def forward(r, s, way):
        return remote(
            rows.at[way, r, s, 1 + way], rows.at[way, r, s, 3], fs.at[way, r, s], fr.at[way, r, s], (y_up, y_dn)[way]
        )

    def hand(r, j, way):
        return remote(
            rows.at[way, r, 2 * j, 3], rows.at[way, r, 2 * j + 1, 3], c3s.at[way, r, j], c3r.at[way, r, j], pair
        )

    def handed(r, s):
        return s % 2 == 1 and (r, s // 2) in HANDED

    cross = remote(s_out, s_mir, cs.at[0], cs.at[1], mirror)

    pl.semaphore_wait(barrier, len(partners))
    steps = [(r, s) for r in range(2) for s in ORDER[r]]
    ready = [s // 2 for s in ORDER[1] if s % 2]
    z_order = [(i, r, s) for i, (r, s) in enumerate(steps) if s > 0 and not (s % 2 and (r, s // 2) in RELAYED)]
    issued = 0

    def issue_z(now):
        nonlocal issued
        while issued < len(z_order):
            i, r, s = z_order[issued]
            if i > now + AHEAD or (r == 1 and now < CROSS_AT):
                break
            z_send(r, s).start()
            issued += 1

    def arrive(i):
        r, s = steps[i]
        if s == 0:
            rows[:, r, 0, 0] = source[r][:, lax.div(z, 2)]
        elif s % 2 and (r, s // 2) in RELAYED:
            relay(r, s // 2).wait_recv()
        else:
            z_send(r, s).wait_recv()
        if s % 2 == 0 and (r, s // 2) in RELAYED:
            relay(r, s // 2).start()
        for way in range(2):
            y_send(r, s, way).start()

    issue_z(0)
    arrive(0)

    loads[2].wait()
    loads[3].wait()
    gather(2, s_out)
    cross.start()

    for c in loads[4:]:
        c.wait()
    for n in range(n_cols):
        wgut[:, n * COLS : (n + 1) * COLS] = wgu[n * COLS : (n + 1) * COLS, :].T
        wdt[n * COLS : (n + 1) * COLS, :] = wd[:, n * COLS : (n + 1) * COLS].T

    def partial_send(c):
        r, k = c // 4, c % 4
        there = (1 - r) * 4 + k
        return remote(ps.at[c], pr.at[there], xs.at[c], xr.at[there], mirror)

    def partial_recv(c):
        return remote(ps.at[c], pr.at[c], xs.at[c], xr.at[c], mirror)

    def products(c):
        r, k = c // 4, c % 4
        gu = dot(rows[0, r, 2 * k : 2 * k + 2].reshape(128, half_width), wgu[...])
        dh = dot(rows[1, r, 2 * k : 2 * k + 2].reshape(128, half_width), wdt[...])
        pf[c, :, 0:256] = gu
        pf[c, :, 256:384] = dh
        ps[c, :, 0:256] = gu.astype(BF16)
        ps[c, :, 256:384] = dh.astype(BF16)
        partial_send(c).start()

    def activations(c):
        r, k = c // 4, c % 4
        partial_recv(c).wait_recv()
        full = pf[c] + pr[c].astype(F32)
        gate, up, dh = full[:, 0:128], full[:, 128:256], full[:, 256:384]
        sig = jax.nn.sigmoid(gate)
        act = gate * sig
        hidden = act * up
        d_gate = dh * up * sig * (1.0 + gate * (1.0 - sig))
        d_up = dh * act
        da[r, 2 * k : 2 * k + 2, :, :, 0:128] = d_gate.astype(BF16).reshape(2, NY, CAP, 128)
        da[r, 2 * k : 2 * k + 2, :, :, 128:256] = d_up.astype(BF16).reshape(2, NY, CAP, 128)
        span = slice(c * 128, (c + 1) * 128)
        dat[0:128, span] = d_gate.T.astype(BF16)
        dat[128:256, span] = d_up.T.astype(BF16)
        dat[256:384, span] = hidden.T.astype(BF16)

    def forward_step(i):
        r, s = steps[i]
        for way in range(2):
            y_send(r, s, way).wait_recv()
            if not handed(r, s):
                forward(r, s, way).start()

    def hand_step(i):
        r, s = steps[i]
        if s % 2 == 0 and (r, s // 2) in HANDED:
            for way in range(2):
                forward(r, s, way).wait_recv()
                hand(r, s // 2, way).start()

    def chunk_done(r, j):
        for way in range(2):
            if (r, j) in HANDED:
                hand(r, j, way).wait_recv()
            else:
                forward(r, 2 * j, way).wait_recv()
                forward(r, 2 * j + 1, way).wait_recv()
        products(r * 4 + j)
        if r == 1:
            activations(4 + j)
            if j != ready[0]:
                activations(ready[ready.index(j) - 1])

    def grad_copies(n):
        here = pl.ds(pl.multiple_of(col + n * COLS, 128), COLS)
        span = pl.ds(n * COLS, COLS)
        pairs = (
            (go_g.at[span, :], gg_h.at[here, :]),
            (go_u.at[span, :], ug_h.at[here, :]),
            (go_d.at[n], dg_h.at[:, here]),
        )
        for j, (src, dst) in enumerate(pairs):
            yield remote(src, dst, gs.at[n, j], gr.at[n, j], mirror), pltpu.make_async_copy(src, dst, gl.at[n, j])

    def grad_recv(n, j):
        there = pl.ds(pl.multiple_of(ocol + n * COLS, 128), COLS)
        span = pl.ds(n * COLS, COLS)
        src, dst = (
            (go_g.at[span, :], gg_h.at[there, :]),
            (go_u.at[span, :], ug_h.at[there, :]),
            (go_d.at[n], dg_h.at[:, there]),
        )[j]
        return remote(src, dst, gs.at[n, j], gr.at[n, j], mirror)

    def grads(n):
        span = slice(n * COLS, (n + 1) * COLS)
        gu = dot(dat[0:256, :], rows[0, :, :, :, :, span].reshape(1024, COLS)).T
        go_g[span, :] = gu[:, 0:128].astype(BF16)
        go_u[span, :] = gu[:, 128:256].astype(BF16)
        go_d[n] = dot(dat[256:384, :], rows[1, :, :, :, :, span].reshape(1024, COLS)).astype(BF16)
        for far, local in grad_copies(n):
            far.start()
            local.start()

    quarter = half_width // 2

    def anti_send(g, way):
        return remote(
            pb.at[:, pl.ds(2 * g, 2), 3, :, pl.ds(way * quarter, quarter)],
            anti.at[way, :, pl.ds(2 * g, 2)],
            ans.at[way, g],
            anr.at[way, g],
            (y_up, y_dn)[way],
        )

    def near_send(g, way):
        return remote(
            pb.at[:, pl.ds(2 * g, 2), 2 - way],
            near.at[way, :, pl.ds(2 * g, 2)],
            ns.at[way, g],
            nr.at[way, g],
            (y_up, y_dn)[way],
        )

    def parts(g):
        span = slice(2 * g, 2 * g + 2)
        lhs = da[:, span].reshape(256, 256)

        def step(n, _):
            part = dot(lhs, wgut[:, cut(n)])
            pb[:, span, :, :, cut(n)] = part.astype(BF16).reshape(2, 2, NY, CAP, COLS)
            return 0

        lax.fori_loop(0, n_cols, step, 0)
        for way in range(2):
            anti_send(g, way).start()

    def nears(g):
        span = slice(2 * g, 2 * g + 2)
        for way in range(2):
            anti_send(g, way).wait_recv()
            part = slice(way * quarter, (way + 1) * quarter)
            total = pb[:, span, 2 - way, :, part].astype(F32) + anti[way, :, span].astype(F32)
            pb[:, span, 2 - way, :, part] = total.astype(BF16)
            near_send(g, way).start()

    def home_send(s):
        j = s // 2
        back = sign * j if s % 2 == 0 else -sign * (1 + j)
        return remote(fin.at[s], home.at[s], hs.at[s], hr.at[s], z_at(back))

    def sums(g):
        span = slice(2 * g, 2 * g + 2)
        for way in range(2):
            near_send(g, way).wait_recv()
        for s in range(2 * g, 2 * g + 2):
            total = pb[:, s, 0].astype(F32) + near[0, :, s].astype(F32) + near[1, :, s].astype(F32)
            if s == 0:
                home[0] = total.astype(BF16)
            else:
                fin[s] = total.astype(BF16)
                home_send(s).start()

    def slot_copies(j):
        _, expert = toward(2 * j)
        dst = so_h.at[expert, :, pl.ds(col, half_width)]
        return (
            pltpu.make_async_copy(slots.at[j], dst, ol.at[1 + j]),
            remote(slots_m.at[j], dst, ss.at[j], sr.at[j], mirror),
        )

    def slot_recv(j):
        _, expert = toward(2 * j)
        return remote(slots_m.at[j], so_h.at[expert, :, pl.ds(ocol, half_width)], ss.at[j], sr.at[j], mirror)

    def gather_home(j):
        for s in (2 * j, 2 * j + 1):
            if s > 0:
                home_send(s).wait_recv()
        both = home[2 * j].astype(F32) + home[2 * j + 1].astype(F32)
        slots_m[j] = both[1].astype(BF16)
        local, far = slot_copies(j)
        far.start()
        slots[j] = both[0].astype(BF16)
        local.start()

    pending = []
    for i in range(len(steps)):
        r, s = steps[i]
        if i > 0:
            arrive(i)
        if i == CROSS_AT:
            cross.wait_recv()
        issue_z(i)
        if i >= 1:
            forward_step(i - 1)
        if i >= 2:
            hand_step(i - 2)
        if s % 2 == 1:
            pending.append((i + (3 if (r, s // 2) in HANDED else 2), r, s // 2))
        while pending and pending[0][0] <= i:
            _, r, j = pending.pop(0)
            chunk_done(r, j)
    forward_step(15)
    hand_step(14)
    parts(ready[0])
    while len(pending) > 1:
        chunk_done(*pending.pop(0)[1:])
    parts(ready[1])
    chunk_done(*pending.pop(0)[1:])
    nears(ready[0])
    activations(ready[3])
    grads(0)
    parts(ready[2])
    nears(ready[1])
    grads(1)
    sums(ready[0])
    parts(ready[3])
    nears(ready[2])
    grads(2)
    sums(ready[1])
    gather_home(ready[0])
    nears(ready[3])
    grads(3)
    grads(4)
    sums(ready[2])
    gather_home(ready[1])
    grads(5)
    grads(6)
    sums(ready[3])
    gather_home(ready[2])
    gather_home(ready[3])

    for n in range(n_cols):
        for j in range(3):
            grad_recv(n, j).wait_recv()
        for far, local in grad_copies(n):
            far.wait_send()
            local.wait()
    for r, s in steps:
        if s % 2 and (r, s // 2) in RELAYED:
            relay(r, s // 2).wait_send()
        elif s > 0:
            z_send(r, s).wait_send()
        for way in range(2):
            y_send(r, s, way).wait_send()
            if not handed(r, s):
                forward(r, s, way).wait_send()
            if s % 2 == 0 and (r, s // 2) in HANDED:
                hand(r, s // 2, way).wait_send()
    for c in range(8):
        partial_send(c).wait_send()
    for g in range(4):
        for way in range(2):
            anti_send(g, way).wait_send()
            near_send(g, way).wait_send()
    for s in range(1, NZ):
        home_send(s).wait_send()
    cross.wait_send()
    save.wait()
    for j in range(4):
        local, far = slot_copies(j)
        far.wait_send()
        local.wait()
        slot_recv(j).wait_recv()


def finish(slots, pmat_t, gate, up, down, ig, gate_o, up_o, down_o):
    ig[...] = dot(pmat_t[:, 0 : EF * CAP], slots[...]).astype(BF16)
    gate_o[...] = gate[...]
    up_o[...] = up[...]
    down_o[...] = down[...]


def body(layer_input, out_grad, combine_weights, expert_ids, w_gate, w_up, w_down):
    tokens, width = layer_input.shape[1:]
    h = width // 2
    n_cols = h // COLS
    dma = pltpu.SemaphoreType.DMA
    outs = pl.pallas_call(
        kernel,
        out_shape=(
            jax.ShapeDtypeStruct((EF, CAP, width), BF16),
            jax.ShapeDtypeStruct((tokens, 128), BF16),
            jax.ShapeDtypeStruct((width, 128), BF16),
            jax.ShapeDtypeStruct((width, 128), BF16),
            jax.ShapeDtypeStruct((128, width), BF16),
        ),
        in_specs=[VMEM, VMEM, ANY, ANY, ANY, ANY, ANY],
        out_specs=(ANY, ANY, ANY, ANY, ANY),
        scratch_shapes=[
            pltpu.VMEM((4, tokens, h), BF16),
            pltpu.VMEM((h, 256), BF16),
            pltpu.VMEM((128, h), BF16),
            pltpu.VMEM((256, h), BF16),
            pltpu.VMEM((h, 128), BF16),
            pltpu.VMEM((128, tokens), BF16),
            pltpu.VMEM((tokens, 128), BF16),
            pltpu.VMEM((128, 1), F32),
            pltpu.VMEM((2, EF, CAP, h), BF16),
            pltpu.VMEM((2, EF, CAP, h), BF16),
            pltpu.VMEM((2, EF, CAP, h), BF16),
            pltpu.VMEM((2, 2, NZ, NY, CAP, h), BF16),
            pltpu.VMEM((8, 128, 384), F32),
            pltpu.VMEM((8, 128, 384), BF16),
            pltpu.VMEM((8, 128, 384), BF16),
            pltpu.VMEM((2, NZ, NY, CAP, 256), BF16),
            pltpu.VMEM((384, 1024), BF16),
            pltpu.VMEM((h, 128), BF16),
            pltpu.VMEM((h, 128), BF16),
            pltpu.VMEM((n_cols, 128, COLS), BF16),
            pltpu.VMEM((2, NZ, NY, CAP, h), BF16),
            pltpu.VMEM((2, 2, NZ, CAP, h // 2), BF16),
            pltpu.VMEM((2, 2, NZ, CAP, h), BF16),
            pltpu.VMEM((NZ, 2, CAP, h), BF16),
            pltpu.VMEM((NZ, 2, CAP, h), BF16),
            pltpu.VMEM((EF, CAP, h), BF16),
            pltpu.VMEM((EF, CAP, h), BF16),
            dma((7,)),
            dma((2, NZ)),
            dma((2, NZ)),
            dma((2, 4)),
            dma((2, 4)),
            dma((2, 2, 4)),
            dma((2, 2, 4)),
            dma((2, 2, NZ)),
            dma((2, 2, NZ)),
            dma((2, 2, NZ)),
            dma((2, 2, NZ)),
            dma((8,)),
            dma((8,)),
            dma((2,)),
            dma((4,)),
            dma((4,)),
            dma((2, 4)),
            dma((2, 4)),
            dma((2, 4)),
            dma((2, 4)),
            dma((NZ,)),
            dma((NZ,)),
            dma((n_cols, 3)),
            dma((n_cols, 3)),
            dma((n_cols, 3)),
            dma((5,)),
        ],
        compiler_params=pltpu.CompilerParams(
            collective_id=0, has_side_effects=True, vmem_limit_bytes=56 * 1024 * 1024
        ),
    )(
        expert_ids[0].T,
        combine_weights[0].T,
        layer_input[0],
        out_grad[0],
        w_gate[0],
        w_up[0],
        w_down[0],
    )
    slots, pmat_t, gate, up, down = outs
    block = width // 2
    results = pl.pallas_call(
        finish,
        grid=(width // block,),
        out_shape=(
            jax.ShapeDtypeStruct((tokens, width), BF16),
            jax.ShapeDtypeStruct((width, 128), BF16),
            jax.ShapeDtypeStruct((width, 128), BF16),
            jax.ShapeDtypeStruct((128, width), BF16),
        ),
        in_specs=[
            pl.BlockSpec((EF * CAP, block), lambda i: (0, i)),
            pl.BlockSpec((tokens, 128), lambda i: (0, 0)),
            pl.BlockSpec((block, 128), lambda i: (i, 0)),
            pl.BlockSpec((block, 128), lambda i: (i, 0)),
            pl.BlockSpec((128, block), lambda i: (0, i)),
        ],
        out_specs=(
            pl.BlockSpec((tokens, block), lambda i: (0, i)),
            pl.BlockSpec((block, 128), lambda i: (i, 0)),
            pl.BlockSpec((block, 128), lambda i: (i, 0)),
            pl.BlockSpec((128, block), lambda i: (0, i)),
        ),
    )(slots.reshape(EF * CAP, width), pmat_t, gate, up, down)
    return tuple(o[None] for o in results)


def solution(mesh):
    return jax.shard_map(
        body,
        mesh=mesh,
        in_specs=(
            P("pipe", "expert", None),
            P("pipe", "expert", None),
            P("pipe", "expert", None),
            P("pipe", "expert", None),
            P("pipe", None, "expert"),
            P("pipe", None, "expert"),
            P("pipe", "expert", None),
        ),
        out_specs=(
            P("pipe", "expert", None),
            P("pipe", None, "expert"),
            P("pipe", None, "expert"),
            P("pipe", "expert", None),
        ),
        check_vma=False,
    )
```

```python
import jax
import jax.numpy as jnp
from jax import lax
from jax.experimental import pallas as pl
from jax.experimental.pallas import tpu as pltpu
from jax.sharding import PartitionSpec as P

MESH = pl.DeviceIdType.MESH
BF16 = jnp.bfloat16
F32 = jnp.float32

NY = 4
NZ = 8
EF = 4
AHEAD = 3
CROSS_AT = 6
LAG = 3
HANDED = ((0, 0), (0, 1), (0, 2), (0, 3), (1, 1), (1, 2))
RELAYED = ((0, 2), (0, 3), (1, 2), (1, 3))
ORDER = ((0, 2, 1, 4, 3, 6, 5, 7), (2, 4, 3, 6, 5, 0, 7, 1))
CAP = 16
COLS = 256
ANY = pl.BlockSpec(memory_space=pl.ANY)
VMEM = pl.BlockSpec(memory_space=pltpu.VMEM)


def dot(a, b):
    return jnp.dot(a, b, preferred_element_type=F32)


def kernel(
    ids,
    probs,
    x_h,
    g_h,
    wg_h,
    wu_h,
    wd_h,
    so_h,
    pm_h,
    gg_h,
    ug_h,
    dg_h,
    tok,
    wgu,
    wd,
    wgut,
    wdt,
    pmat,
    pmat_t,
    wslot,
    s_own,
    s_mir,
    s_out,
    rows,
    pf,
    ps,
    pr,
    da,
    dat,
    go_g,
    go_u,
    go_d,
    pb,
    anti,
    near,
    fin,
    home,
    slots,
    slots_m,
    lsem,
    zs,
    zr,
    c0s,
    c0r,
    c3s,
    c3r,
    ys,
    yr,
    fs,
    fr,
    xs,
    xr,
    cs,
    ss,
    sr,
    ans,
    anr,
    ns,
    nr,
    hs,
    hr,
    gs,
    gr,
    gl,
    ol,
):
    n_pipe = lax.axis_size("pipe")
    p = lax.axis_index("pipe")
    ex = lax.axis_index("expert")
    z = lax.div(ex, NY)
    y = lax.rem(ex, NY)
    tokens, half_width = tok.shape[1], tok.shape[2]
    n_cols = half_width // COLS
    half = lax.div(p, n_pipe // 2)
    col = pl.multiple_of(half * half_width, 128)
    ocol = pl.multiple_of((1 - half) * half_width, 128)
    mirror = (n_pipe - 1 - p, ex)
    y_up = (p, z * NY + lax.rem(y + 1, NY))
    y_dn = (p, z * NY + lax.rem(y + NY - 1, NY))

    odd = lax.rem(z, 2)
    sign = 2 * odd - 1

    def z_at(delta):
        return (p, lax.rem(z + delta + NZ, NZ) * NY + y)

    pair = z_at(-sign)

    def toward(s):
        delta = (1 - 2 * lax.rem(z + s // 2, 2)) * (s // 2 + s % 2)
        return delta, lax.div(lax.rem(z + delta + NZ, NZ), 2)

    def remote(src, dst, send, recv, device):
        return pltpu.make_async_remote_copy(
            src_ref=src, dst_ref=dst, send_sem=send, recv_sem=recv, device_id=device, device_id_type=MESH
        )

    def cut(n):
        return pl.ds(pl.multiple_of(n * COLS, COLS), COLS)

    loads = [
        pltpu.make_async_copy(x_h.at[:, pl.ds(col, half_width)], tok.at[0], lsem.at[0]),
        pltpu.make_async_copy(g_h.at[:, pl.ds(col, half_width)], tok.at[1], lsem.at[1]),
        pltpu.make_async_copy(x_h.at[:, pl.ds(ocol, half_width)], tok.at[2], lsem.at[2]),
        pltpu.make_async_copy(g_h.at[:, pl.ds(ocol, half_width)], tok.at[3], lsem.at[3]),
        pltpu.make_async_copy(wg_h.at[pl.ds(col, half_width), :], wgu.at[:, pl.ds(0, 128)], lsem.at[4]),
        pltpu.make_async_copy(wu_h.at[pl.ds(col, half_width), :], wgu.at[:, pl.ds(128, 128)], lsem.at[5]),
        pltpu.make_async_copy(wd_h.at[:, pl.ds(col, half_width)], wd, lsem.at[6]),
    ]
    for c in loads:
        c.start()

    barrier = pltpu.get_barrier_semaphore()
    partners = [mirror, y_up, y_dn] + [z_at(d) for d in range(1, NZ)]
    for device in partners:
        pl.semaphore_signal(barrier, inc=1, device_id=device, device_id_type=MESH)

    row = lax.broadcasted_iota(jnp.int32, (128, tokens), 0)
    row_expert = lax.div(row, CAP)
    named = jnp.zeros((128, tokens), F32)
    weight = jnp.zeros((128, tokens), F32)
    for k in range(ids.shape[0]):
        hit = ids[k : k + 1, :] == row_expert
        named = jnp.where(hit, 1.0, named)
        weight = jnp.where(hit, probs[k : k + 1, :], weight)
    named = jnp.where(row < EF * CAP, named, 0.0)
    before = (
        lax.broadcasted_iota(jnp.int32, (tokens, tokens), 0) < lax.broadcasted_iota(jnp.int32, (tokens, tokens), 1)
    ).astype(F32)
    count = dot(named.astype(BF16), before.astype(BF16))
    placed = jnp.where(count == lax.rem(row, CAP).astype(F32), named, 0.0)
    pmat[...] = placed.astype(BF16)
    pmat_t[...] = placed.T.astype(BF16)
    wslot[...] = jnp.sum(placed * weight, axis=1, keepdims=True)
    save = pltpu.make_async_copy(pmat_t, pm_h, ol.at[0])
    save.start()

    def gather(base, dst):
        def step(n, _):
            x_rows = dot(pmat[0 : EF * CAP, :], tok[base, :, cut(n)])
            dst[0, :, :, cut(n)] = x_rows.astype(BF16).reshape(EF, CAP, COLS)
            g_rows = dot(pmat[0 : EF * CAP, :], tok[base + 1, :, cut(n)]) * wslot[0 : EF * CAP, :]
            dst[1, :, :, cut(n)] = g_rows.astype(BF16).reshape(EF, CAP, COLS)
            return 0

        lax.fori_loop(0, n_cols, step, 0)

    loads[0].wait()
    loads[1].wait()
    gather(0, s_own)

    source = (s_own, s_mir)

    def z_send(r, s):
        delta, expert = toward(s)
        return remote(source[r].at[:, expert], rows.at[:, r, s, 0], zs.at[r, s], zr.at[r, s], z_at(delta))

    def relay(r, j):
        return remote(rows.at[:, r, 2 * j, 0], rows.at[:, r, 2 * j + 1, 0], c0s.at[r, j], c0r.at[r, j], pair)

    def y_send(r, s, way):
        return remote(
            rows.at[:, r, s, 0], rows.at[:, r, s, 1 + way], ys.at[way, r, s], yr.at[way, r, s], (y_up, y_dn)[way]
        )

    def forward(r, s, way):
        return remote(
            rows.at[way, r, s, 1 + way], rows.at[way, r, s, 3], fs.at[way, r, s], fr.at[way, r, s], (y_up, y_dn)[way]
        )

    def hand(r, j, way):
        return remote(
            rows.at[way, r, 2 * j, 3], rows.at[way, r, 2 * j + 1, 3], c3s.at[way, r, j], c3r.at[way, r, j], pair
        )

    def handed(r, s):
        return s % 2 == 1 and (r, s // 2) in HANDED

    cross = remote(s_out, s_mir, cs.at[0], cs.at[1], mirror)

    pl.semaphore_wait(barrier, len(partners))
    steps = [(r, s) for r in range(2) for s in ORDER[r]]
    ready = [s // 2 for s in ORDER[1] if s % 2]
    z_order = [(i, r, s) for i, (r, s) in enumerate(steps) if s > 0 and not (s % 2 and (r, s // 2) in RELAYED)]
    issued = 0

    def issue_z(now):
        nonlocal issued
        while issued < len(z_order):
            i, r, s = z_order[issued]
            if i > now + AHEAD or (r == 1 and now < CROSS_AT):
                break
            z_send(r, s).start()
            issued += 1

    def arrive(i):
        r, s = steps[i]
        if s == 0:
            rows[:, r, 0, 0] = source[r][:, lax.div(z, 2)]
        elif s % 2 and (r, s // 2) in RELAYED:
            relay(r, s // 2).wait_recv()
        else:
            z_send(r, s).wait_recv()
        if s % 2 == 0 and (r, s // 2) in RELAYED:
            relay(r, s // 2).start()
        for way in range(2):
            y_send(r, s, way).start()

    issue_z(0)
    arrive(0)

    loads[2].wait()
    loads[3].wait()
    gather(2, s_out)
    cross.start()

    for c in loads[4:]:
        c.wait()
    for n in range(n_cols):
        wgut[:, n * COLS : (n + 1) * COLS] = wgu[n * COLS : (n + 1) * COLS, :].T
        wdt[n * COLS : (n + 1) * COLS, :] = wd[:, n * COLS : (n + 1) * COLS].T

    def partial_copy(c, there, first, count):
        span = pl.ds(first, count)
        k = first // 64
        return remote(ps.at[c, span], pr.at[there, span], xs.at[c, k], xr.at[there, k], mirror)

    def spans(c):
        return ((0, 64), (64, 64)) if c % 4 == ready[3] and c >= 4 else ((0, 128),)

    def partial_send(c, first, count):
        return partial_copy(c, (c + 4) % 8, first, count)

    def products(c, first=0, count=128):
        r, k = c // 4, c % 4
        slot = slice(2 * k + first // 64, 2 * k + (first + count) // 64)
        gu = dot(rows[0, r, slot].reshape(count, half_width), wgu[...])
        dh = dot(rows[1, r, slot].reshape(count, half_width), wdt[...])
        span = slice(first, first + count)
        pf[c, span, 0:256] = gu
        pf[c, span, 256:384] = dh
        ps[c, span, 0:256] = gu.astype(BF16)
        ps[c, span, 256:384] = dh.astype(BF16)
        partial_send(c, first, count).start()

    def activations(c):
        r, k = c // 4, c % 4
        for first, count in spans((c + 4) % 8):
            partial_copy(c, c, first, count).wait_recv()
        full = pf[c] + pr[c].astype(F32)
        gate, up, dh = full[:, 0:128], full[:, 128:256], full[:, 256:384]
        sig = jax.nn.sigmoid(gate)
        act = gate * sig
        hidden = act * up
        d_gate = dh * up * sig * (1.0 + gate * (1.0 - sig))
        d_up = dh * act
        da[r, 2 * k : 2 * k + 2, :, :, 0:128] = d_gate.astype(BF16).reshape(2, NY, CAP, 128)
        da[r, 2 * k : 2 * k + 2, :, :, 128:256] = d_up.astype(BF16).reshape(2, NY, CAP, 128)
        span = slice(c * 128, (c + 1) * 128)
        dat[0:128, span] = d_gate.T.astype(BF16)
        dat[128:256, span] = d_up.T.astype(BF16)
        dat[256:384, span] = hidden.T.astype(BF16)

    def forward_step(i):
        r, s = steps[i]
        for way in range(2):
            y_send(r, s, way).wait_recv()
            if not handed(r, s):
                forward(r, s, way).start()

    def hand_step(i):
        r, s = steps[i]
        if s % 2 == 0 and (r, s // 2) in HANDED:
            for way in range(2):
                forward(r, s, way).wait_recv()
                hand(r, s // 2, way).start()

    def rows_done(r, s):
        for way in range(2):
            if handed(r, s):
                hand(r, s // 2, way).wait_recv()
            elif (r, s // 2) not in HANDED:
                forward(r, s, way).wait_recv()

    def chunk_done(r, j):
        rows_done(r, 2 * j)
        rows_done(r, 2 * j + 1)
        products(r * 4 + j)
        if r == 1:
            activations(4 + j)
            if j != ready[0]:
                activations(ready[ready.index(j) - 1])

    def grad_copies(n):
        here = pl.ds(pl.multiple_of(col + n * COLS, 128), COLS)
        span = pl.ds(n * COLS, COLS)
        pairs = (
            (go_g.at[span, :], gg_h.at[here, :]),
            (go_u.at[span, :], ug_h.at[here, :]),
            (go_d.at[n], dg_h.at[:, here]),
        )
        for j, (src, dst) in enumerate(pairs):
            yield remote(src, dst, gs.at[n, j], gr.at[n, j], mirror), pltpu.make_async_copy(src, dst, gl.at[n, j])

    def grad_recv(n, j):
        there = pl.ds(pl.multiple_of(ocol + n * COLS, 128), COLS)
        span = pl.ds(n * COLS, COLS)
        src, dst = (
            (go_g.at[span, :], gg_h.at[there, :]),
            (go_u.at[span, :], ug_h.at[there, :]),
            (go_d.at[n], dg_h.at[:, there]),
        )[j]
        return remote(src, dst, gs.at[n, j], gr.at[n, j], mirror)

    def grads(n):
        span = slice(n * COLS, (n + 1) * COLS)
        gu = dot(dat[0:256, :], rows[0, :, :, :, :, span].reshape(1024, COLS)).T
        go_g[span, :] = gu[:, 0:128].astype(BF16)
        go_u[span, :] = gu[:, 128:256].astype(BF16)
        go_d[n] = dot(dat[256:384, :], rows[1, :, :, :, :, span].reshape(1024, COLS)).astype(BF16)
        for far, local in grad_copies(n):
            far.start()
            local.start()

    quarter = half_width // 2

    def anti_send(g, way):
        return remote(
            pb.at[:, pl.ds(2 * g, 2), 3, :, pl.ds(way * quarter, quarter)],
            anti.at[way, :, pl.ds(2 * g, 2)],
            ans.at[way, g],
            anr.at[way, g],
            (y_up, y_dn)[way],
        )

    def near_send(g, way):
        return remote(
            pb.at[:, pl.ds(2 * g, 2), 2 - way],
            near.at[way, :, pl.ds(2 * g, 2)],
            ns.at[way, g],
            nr.at[way, g],
            (y_up, y_dn)[way],
        )

    def parts(g):
        span = slice(2 * g, 2 * g + 2)
        lhs = da[:, span].reshape(256, 256)

        def step(n, _):
            part = dot(lhs, wgut[:, cut(n)])
            pb[:, span, :, :, cut(n)] = part.astype(BF16).reshape(2, 2, NY, CAP, COLS)
            return 0

        lax.fori_loop(0, n_cols, step, 0)
        for way in range(2):
            anti_send(g, way).start()

    def nears(g):
        span = slice(2 * g, 2 * g + 2)
        for way in range(2):
            anti_send(g, way).wait_recv()
            part = slice(way * quarter, (way + 1) * quarter)
            total = pb[:, span, 2 - way, :, part].astype(F32) + anti[way, :, span].astype(F32)
            pb[:, span, 2 - way, :, part] = total.astype(BF16)
            near_send(g, way).start()

    def home_send(s):
        j = s // 2
        back = sign * j if s % 2 == 0 else -sign * (1 + j)
        return remote(fin.at[s], home.at[s], hs.at[s], hr.at[s], z_at(back))

    def sums(g):
        span = slice(2 * g, 2 * g + 2)
        for way in range(2):
            near_send(g, way).wait_recv()
        for s in range(2 * g, 2 * g + 2):
            total = pb[:, s, 0].astype(F32) + near[0, :, s].astype(F32) + near[1, :, s].astype(F32)
            if s == 0:
                home[0] = total.astype(BF16)
            else:
                fin[s] = total.astype(BF16)
                home_send(s).start()

    def slot_copies(j):
        _, expert = toward(2 * j)
        dst = so_h.at[expert, :, pl.ds(col, half_width)]
        return (
            pltpu.make_async_copy(slots.at[j], dst, ol.at[1 + j]),
            remote(slots_m.at[j], dst, ss.at[j], sr.at[j], mirror),
        )

    def slot_recv(j):
        _, expert = toward(2 * j)
        return remote(slots_m.at[j], so_h.at[expert, :, pl.ds(ocol, half_width)], ss.at[j], sr.at[j], mirror)

    def gather_home(j):
        for s in (2 * j, 2 * j + 1):
            if s > 0:
                home_send(s).wait_recv()
        both = home[2 * j].astype(F32) + home[2 * j + 1].astype(F32)
        slots_m[j] = both[1].astype(BF16)
        local, far = slot_copies(j)
        far.start()
        slots[j] = both[0].astype(BF16)
        local.start()

    pending = []
    for i in range(len(steps) + LAG):
        if i < len(steps):
            r, s = steps[i]
            if i > 0:
                arrive(i)
            if i == CROSS_AT:
                cross.wait_recv()
            issue_z(i)
            if s % 2 == 1:
                pending.append((i + LAG + (2 if (r, s // 2) in HANDED else 1), r, s // 2))
        if i >= LAG:
            forward_step(i - LAG)
        if i >= LAG + 1:
            hand_step(i - LAG - 1)
        while len(pending) > 1 and pending[0][0] <= i:
            chunk_done(*pending.pop(0)[1:])
    final = ready[3]
    parts(ready[0])
    while len(pending) > 1:
        chunk_done(*pending.pop(0)[1:])
    parts(ready[1])
    rows_done(1, 2 * final)
    products(4 + final, 0, 64)
    rows_done(1, 2 * final + 1)
    products(4 + final, 64, 64)
    activations(4 + final)
    activations(ready[2])
    parts(ready[2])
    nears(ready[0])
    activations(final)
    parts(final)
    grads(0)
    nears(ready[1])
    grads(1)
    nears(ready[2])
    grads(2)
    sums(ready[0])
    nears(final)
    grads(3)
    sums(ready[1])
    grads(4)
    gather_home(ready[0])
    sums(ready[2])
    grads(5)
    gather_home(ready[1])
    grads(6)
    sums(final)
    gather_home(ready[2])
    gather_home(final)

    for n in range(n_cols):
        for j in range(3):
            grad_recv(n, j).wait_recv()
        for far, local in grad_copies(n):
            far.wait_send()
            local.wait()
    for r, s in steps:
        if s % 2 and (r, s // 2) in RELAYED:
            relay(r, s // 2).wait_send()
        elif s > 0:
            z_send(r, s).wait_send()
        for way in range(2):
            y_send(r, s, way).wait_send()
            if not handed(r, s):
                forward(r, s, way).wait_send()
            if s % 2 == 0 and (r, s // 2) in HANDED:
                hand(r, s // 2, way).wait_send()
    for c in range(8):
        for first, count in spans(c):
            partial_send(c, first, count).wait_send()
    for g in range(4):
        for way in range(2):
            anti_send(g, way).wait_send()
            near_send(g, way).wait_send()
    for s in range(1, NZ):
        home_send(s).wait_send()
    cross.wait_send()
    save.wait()
    for j in range(4):
        local, far = slot_copies(j)
        far.wait_send()
        local.wait()
        slot_recv(j).wait_recv()


def finish(slots, pmat_t, gate, up, down, ig, gate_o, up_o, down_o):
    ig[...] = dot(pmat_t[:, 0 : EF * CAP], slots[...]).astype(BF16)
    gate_o[...] = gate[...]
    up_o[...] = up[...]
    down_o[...] = down[...]


def body(layer_input, out_grad, combine_weights, expert_ids, w_gate, w_up, w_down):
    tokens, width = layer_input.shape[1:]
    h = width // 2
    n_cols = h // COLS
    dma = pltpu.SemaphoreType.DMA
    outs = pl.pallas_call(
        kernel,
        out_shape=(
            jax.ShapeDtypeStruct((EF, CAP, width), BF16),
            jax.ShapeDtypeStruct((tokens, 128), BF16),
            jax.ShapeDtypeStruct((width, 128), BF16),
            jax.ShapeDtypeStruct((width, 128), BF16),
            jax.ShapeDtypeStruct((128, width), BF16),
        ),
        in_specs=[VMEM, VMEM, ANY, ANY, ANY, ANY, ANY],
        out_specs=(ANY, ANY, ANY, ANY, ANY),
        scratch_shapes=[
            pltpu.VMEM((4, tokens, h), BF16),
            pltpu.VMEM((h, 256), BF16),
            pltpu.VMEM((128, h), BF16),
            pltpu.VMEM((256, h), BF16),
            pltpu.VMEM((h, 128), BF16),
            pltpu.VMEM((128, tokens), BF16),
            pltpu.VMEM((tokens, 128), BF16),
            pltpu.VMEM((128, 1), F32),
            pltpu.VMEM((2, EF, CAP, h), BF16),
            pltpu.VMEM((2, EF, CAP, h), BF16),
            pltpu.VMEM((2, EF, CAP, h), BF16),
            pltpu.VMEM((2, 2, NZ, NY, CAP, h), BF16),
            pltpu.VMEM((8, 128, 384), F32),
            pltpu.VMEM((8, 128, 384), BF16),
            pltpu.VMEM((8, 128, 384), BF16),
            pltpu.VMEM((2, NZ, NY, CAP, 256), BF16),
            pltpu.VMEM((384, 1024), BF16),
            pltpu.VMEM((h, 128), BF16),
            pltpu.VMEM((h, 128), BF16),
            pltpu.VMEM((n_cols, 128, COLS), BF16),
            pltpu.VMEM((2, NZ, NY, CAP, h), BF16),
            pltpu.VMEM((2, 2, NZ, CAP, h // 2), BF16),
            pltpu.VMEM((2, 2, NZ, CAP, h), BF16),
            pltpu.VMEM((NZ, 2, CAP, h), BF16),
            pltpu.VMEM((NZ, 2, CAP, h), BF16),
            pltpu.VMEM((EF, CAP, h), BF16),
            pltpu.VMEM((EF, CAP, h), BF16),
            dma((7,)),
            dma((2, NZ)),
            dma((2, NZ)),
            dma((2, 4)),
            dma((2, 4)),
            dma((2, 2, 4)),
            dma((2, 2, 4)),
            dma((2, 2, NZ)),
            dma((2, 2, NZ)),
            dma((2, 2, NZ)),
            dma((2, 2, NZ)),
            dma((8, 2)),
            dma((8, 2)),
            dma((2,)),
            dma((4,)),
            dma((4,)),
            dma((2, 4)),
            dma((2, 4)),
            dma((2, 4)),
            dma((2, 4)),
            dma((NZ,)),
            dma((NZ,)),
            dma((n_cols, 3)),
            dma((n_cols, 3)),
            dma((n_cols, 3)),
            dma((5,)),
        ],
        compiler_params=pltpu.CompilerParams(
            collective_id=0, has_side_effects=True, vmem_limit_bytes=56 * 1024 * 1024
        ),
    )(
        expert_ids[0].T,
        combine_weights[0].T,
        layer_input[0],
        out_grad[0],
        w_gate[0],
        w_up[0],
        w_down[0],
    )
    slots, pmat_t, gate, up, down = outs
    block = width // 2
    results = pl.pallas_call(
        finish,
        grid=(width // block,),
        out_shape=(
            jax.ShapeDtypeStruct((tokens, width), BF16),
            jax.ShapeDtypeStruct((width, 128), BF16),
            jax.ShapeDtypeStruct((width, 128), BF16),
            jax.ShapeDtypeStruct((128, width), BF16),
        ),
        in_specs=[
            pl.BlockSpec((EF * CAP, block), lambda i: (0, i)),
            pl.BlockSpec((tokens, 128), lambda i: (0, 0)),
            pl.BlockSpec((block, 128), lambda i: (i, 0)),
            pl.BlockSpec((block, 128), lambda i: (i, 0)),
            pl.BlockSpec((128, block), lambda i: (0, i)),
        ],
        out_specs=(
            pl.BlockSpec((tokens, block), lambda i: (0, i)),
            pl.BlockSpec((block, 128), lambda i: (i, 0)),
            pl.BlockSpec((block, 128), lambda i: (i, 0)),
            pl.BlockSpec((128, block), lambda i: (0, i)),
        ),
    )(slots.reshape(EF * CAP, width), pmat_t, gate, up, down)
    return tuple(o[None] for o in results)


def solution(mesh):
    return jax.shard_map(
        body,
        mesh=mesh,
        in_specs=(
            P("pipe", "expert", None),
            P("pipe", "expert", None),
            P("pipe", "expert", None),
            P("pipe", "expert", None),
            P("pipe", None, "expert"),
            P("pipe", None, "expert"),
            P("pipe", "expert", None),
        ),
        out_specs=(
            P("pipe", "expert", None),
            P("pipe", None, "expert"),
            P("pipe", None, "expert"),
            P("pipe", "expert", None),
        ),
        check_vma=False,
    )
```
